512 devices in a mesh: dp: 16 (over z), seq: 32 (over x, y, core).
Axes of the slice: x: 4, y: 4, z: 16, core: 2. Of those that a mesh axis runs over, the one named last changes fastest.
Arguments:
- tokens: float32 [16, 4096, 2048], P('dp', 'seq'), may hold values from -10 to 10, as said below
- cotangent: float32 [16, 4096, 2048], P('dp', 'seq'), may hold values from -6 to 6
- short_weights: float32 [3, 8, 2048], replicated, may hold values from 0.2 to 0.6
Outputs:
- grad_tokens: float32 [16, 4096, 2048], P('dp', 'seq')
- grad_weights: float32 [3, 8, 2048], P(None, None, 'seq')
The draws below stay inside these ranges and needn't reach their ends.
Inputs may be any that keep to these rules, and one draw needn't show every extreme that they name: `tokens`: Real-valued activations of order one.
All inputs are finite; a program needn't handle non-finite values.
Results may differ from the reference program's by a relative error of at most 0.0003.
Values sent between devices are 32-bit elements; how exact they have to be, the bound alone decides.
A program may use at most 64 MiB of HBM per device.

```python
import jax
import jax.numpy as jnp
from jax import lax

HEADS = 32
HEAD = 64
D = 2048
K = 8
LENGTH = 4096
SUMS = 512
SEQS = 16


def draw_tokens(key, part):
    base_key = jax.random.fold_in(key, 11)
    shape = (SEQS, LENGTH, D)
    base = jax.random.normal(base_key, shape, jnp.float32)
    return jnp.clip(base, -6.0, 6.0).astype(jnp.float32)


def steps_of(stream_key, shape, cuts, low, largest):
    loudness = 1.0
    for axis_at, blocks in cuts:
        draws = jax.random.uniform(jax.random.fold_in(jax.random.fold_in(stream_key, 6), axis_at), (blocks,), jnp.float32, low / len(cuts), largest / len(cuts))
        loudness = loudness * jnp.repeat(jnp.exp(draws), shape[axis_at] // blocks).reshape((-1,) + (1,) * (len(shape) - 1 - axis_at))
    return loudness


def scatter_about(key, shape, deviation, bound, cuts=(), held_as=jnp.bfloat16):
    array = jax.random.normal(key, shape, jnp.float32) * deviation
    if len(cuts) > 0:
        array = steps_of(key, shape, cuts, -0.22, 0.18) * array
    return jnp.clip(array, min=-bound, max=bound).astype(held_as)


def setup_inputs(seed: int = 0) -> dict:
    arg_keys = jax.random.split(jax.random.key(seed), 4)
    return {
        "tokens": draw_tokens(jax.random.fold_in(arg_keys[3], 71), 0),
        "cotangent": scatter_about(arg_keys[1], (SEQS, LENGTH, D), 1.0, 6.0, ((0, 16), (1, 32)), jnp.float32),
        "short_weights": jnp.clip(jax.random.uniform(arg_keys[2], (3, K, D), jnp.float32, 0.2, 0.6), 0.2, 0.6),
    }


def attend_back(query, key, value, grad_o):
    scale = HEAD ** (-0.5)
    hi = lax.Precision.HIGHEST
    scores = scale * jnp.einsum('qhe,khe->hqk', query, key, precision=hi)
    top = lax.optimization_barrier(jnp.max(scores, axis=-1, keepdims=True))
    expo = jnp.exp(scores - top)
    probs = expo / lax.optimization_barrier(jnp.sum(expo, axis=-1, keepdims=True))
    grad_probs = jnp.einsum('qhe,khe->hqk', grad_o, value, precision=hi)
    delta = lax.optimization_barrier(jnp.sum(probs * grad_probs, axis=-1, keepdims=True))
    grad_scores = probs * (grad_probs - delta)
    grad_q = scale * jnp.einsum('hqk,khe->qhe', grad_scores, key, precision=hi)
    grad_k = scale * jnp.einsum('hqk,qhe->khe', grad_scores, query, precision=hi)
    grad_v = jnp.einsum('hqk,qhe->khe', probs, grad_o, precision=hi)
    return (grad_q, grad_k, grad_v)

def reference(tokens, cotangent, short_weights):
    hi = lax.Precision.HIGHEST

    def one_sequence(pair):
        seq_tokens, seq_grad = pair
        grouped = seq_tokens.reshape(SUMS, K, D)
        summary = jnp.einsum('jic,mic->mjc', grouped, short_weights, precision=hi)
        grad_o = lax.optimization_barrier(jnp.sum(seq_grad.reshape(SUMS, K, D), axis=1))
        shaped = summary.reshape(3, SUMS, HEADS, HEAD)
        grad_q, grad_k, grad_v = attend_back(shaped[0], shaped[1], shaped[2], grad_o.reshape(SUMS, HEADS, HEAD))
        grad_summary = jnp.stack([grad_q, grad_k, grad_v]).reshape(3, SUMS, D)
        grad_in = jnp.einsum('mjc,mic->jic', grad_summary, short_weights, precision=hi).reshape(SUMS * K, D)
        partial_value = jnp.einsum('mjc,jic->mic', grad_summary, grouped, precision=hi)
        return (grad_in, partial_value)
    grad_tokens, partials = lax.map(one_sequence, (tokens, cotangent))
    raw = lax.optimization_barrier(jnp.sum(partials, axis=0))
    mean_sq = jnp.mean(raw * raw)
    factor = jnp.minimum(1.0, 1.0 / jnp.sqrt(mean_sq + 1e-06))
    return (grad_tokens, raw * factor)
```

```python
import functools

import jax
import jax.numpy as jnp
from jax import lax
from jax.experimental import pallas as pl
from jax.experimental.pallas import tpu as pltpu
from jax.sharding import PartitionSpec as P

HEAD = 64
LANES = 128
K = 8
GROUP = 16
SCALE = HEAD ** (-0.5)
LOG2E = 1.4426950408889634
MESH = pl.DeviceIdType.MESH
NT = (((1,), (1,)), ((), ()))
NN = (((1,), (0,)), ((), ()))
F32, BF16 = jnp.float32, jnp.bfloat16


def low_half(shape):
    return lax.broadcasted_iota(jnp.int32, shape, len(shape) - 1) < HEAD


def swap_halves(x):
    return pltpu.roll(x, HEAD, len(x.shape) - 1)


def pair_up(x, y):
    low = low_half(x.shape)
    r = swap_halves(jnp.where(low, y, x))
    return jnp.where(low, x, r), jnp.where(low, r, y)


def both_halves(x):
    low = low_half(x.shape)
    r = swap_halves(x)
    return jnp.where(low, x, r), jnp.where(low, r, x)


def dot(a, b, dims):
    return lax.dot_general(a, b, dims, preferred_element_type=F32)


def two_parts(x):
    high = x.astype(BF16).astype(F32)
    return high, x - high


def main_kernel(
    n_seq, n_dp,
    tok_hbm, cot_hbm, w_hbm,
    out_ref, total_ref, squares_ref,
    tok, cot, w, wb,
    send, recv,
    qs, ks, qc, os, vs, oc, kc, kt,
    acc_k, acc_v, acc_q,
    ret, back, rows, dp_all,
    load_sem, send_sem, in_sem, recv_sem,
):
    me = lax.axis_index("seq")
    plane = lax.axis_index("dp")
    tiles = n_seq // 2
    chip, core = me // 2, lax.rem(me, 2)
    cx, cy = chip // 4, lax.rem(chip, 4)
    sums = n_seq * GROUP
    half = sums // 2

    barrier = pltpu.get_barrier_semaphore()

    def hello_seq(d, _):
        other = lax.rem(me + d, n_seq)
        pl.semaphore_signal(barrier, inc=1, device_id=(plane, other), device_id_type=MESH)
        return 0

    def hello_dp(d, _):
        other = lax.rem(plane + d, n_dp)
        pl.semaphore_signal(barrier, inc=1, device_id=(other, me), device_id_type=MESH)
        return 0

    lax.fori_loop(1, n_seq, hello_seq, 0)
    lax.fori_loop(1, n_dp, hello_dp, 0)

    def tile_loads(t):
        lanes = pl.ds(pl.multiple_of(t * LANES, LANES), LANES)
        return (
            pltpu.make_async_copy(tok_hbm.at[0, :, lanes], tok.at[t], load_sem.at[2 * t]),
            pltpu.make_async_copy(cot_hbm.at[0, :, lanes], cot.at[t], load_sem.at[2 * t + 1]),
        )

    def start_loads(t, _):
        for c in tile_loads(t):
            c.start()
        return 0

    lax.fori_loop(0, tiles, start_loads, 0)
    w_load = pltpu.make_async_copy(w_hbm, w, load_sem.at[2 * tiles])
    w_load.start()

    def pack(t, _):
        for c in tile_loads(t):
            c.wait()
        o = None
        for i in range(K):
            x = tok[t, pl.ds(i, GROUP, stride=K), :]
            c = cot[t, pl.ds(i, GROUP, stride=K), :]
            o = c if o is None else o + c
            even, odd = pair_up(x[:8], x[8:])
            send[2 * t, 8 * i : 8 * i + 8] = even
            send[2 * t + 1, 8 * i : 8 * i + 8] = odd
        even, odd = pair_up(o[:8], o[8:])
        send[2 * t, 8 * K : 8 * K + 8] = even
        send[2 * t + 1, 8 * K : 8 * K + 8] = odd
        return 0

    lax.fori_loop(0, tiles, pack, 0)

    w_load.wait()
    lanes = pl.ds(pl.multiple_of(chip * LANES, LANES), LANES)
    for m in range(3):
        first, second = both_halves(w[m, :, lanes])
        mine = jnp.where(core == 0, first, second)
        for i in range(K):
            wb[K * m + i] = jnp.broadcast_to(mine[i : i + 1], (8, LANES))

    pl.semaphore_wait(barrier, n_seq + n_dp - 2)

    def to_seq(src_of, dst, s, sem_of):
        def one(e, _):
            k = e // 2
            x, y = lax.rem(cx + k // 4, 4), lax.rem(cy + lax.rem(k, 4), 4)
            other = (x * 4 + y) * 2 + lax.rem(core + lax.rem(e, 2), 2)
            pltpu.make_async_remote_copy(
                src_ref=src_of(other),
                dst_ref=dst.at[me],
                send_sem=send_sem.at[s],
                recv_sem=sem_of(k),
                device_id=(plane, other),
                device_id_type=MESH,
            ).start()
            return 0

        lax.fori_loop(1, n_seq, one, 0)

    def arrived(dst, sem):
        pltpu.make_async_copy(dst, dst, sem).wait()

    to_seq(lambda h: send.at[h], recv, 0, lambda k: in_sem.at[k])
    pltpu.make_async_copy(send.at[me], recv.at[me], in_sem.at[0]).start()

    def query_role(x, side, cols, r0):
        for part, r in zip(both_halves(x), (r0, half + r0)):
            h, l = two_parts(part)
            at = pl.ds(pl.multiple_of(r, GROUP), GROUP)
            side[at, :LANES] = h.astype(BF16)
            side[at, LANES:] = l.astype(BF16)
            cols[at, :] = jnp.where(low_half(h.shape), h, l).astype(BF16)

    def key_role(x, side, r0, keep=None):
        for part, r in zip(both_halves(x), (r0, half + r0)):
            h, l = two_parts(part)
            at = pl.ds(pl.multiple_of(r, GROUP), GROUP)
            c = jnp.where(low_half(h.shape), h, l)
            side[at, :LANES] = c.astype(BF16)
            side[at, LANES:] = c.astype(BF16)
            if keep is not None:
                keep[at, :] = c

    def take(k, _):
        x, y = lax.rem(cx + 4 - k // 4, 4), lax.rem(cy + 4 - lax.rem(k, 4), 4)
        c = x * 4 + y
        block = recv.at[pl.ds(2 * c, 2)]
        arrived(block, in_sem.at[k])
        pooled = []
        for m in range(3):
            s = None
            for i in range(K):
                a = recv[pl.ds(2 * c, 2), 8 * i : 8 * i + 8, :] * wb[K * m + i]
                s = a if s is None else s + a
            pooled.append(s.reshape(GROUP, LANES))
        o = recv[pl.ds(2 * c, 2), 8 * K : 8 * K + 8, :].reshape(GROUP, LANES)
        r0 = c * GROUP
        query_role(pooled[0], qs, qc, r0)
        key_role(pooled[1], ks, r0, kc)
        key_role(pooled[2], vs, r0)
        query_role(o, os, oc, r0)
        return 0

    lax.fori_loop(0, tiles, take, 0)

    kt[...] = kc[...].T.astype(BF16)
    for b in range(2):
        cols = slice(b * half, (b + 1) * half)
        s = dot(ks[...], qs[cols, :], NT)
        top = jnp.max(s, axis=0, keepdims=True)
        e = jnp.exp2((s - top) * (SCALE * LOG2E))
        p = e * (1.0 / jnp.sum(e, axis=0, keepdims=True))
        gp = dot(vs[...], os[cols, :], NT)
        delta = jnp.sum(p * gp, axis=0, keepdims=True)
        gs = p * (gp - delta)
        p_high, p_low = (x.astype(BF16) for x in two_parts(p))
        g_high, g_low = (x.astype(BF16) for x in two_parts(gs))
        gv = dot(p_high, oc[cols, :], NN) + dot(p_low, oc[cols, :], NN)
        gk = dot(g_high, qc[cols, :], NN) + dot(g_low, qc[cols, :], NN)
        if b == 0:
            acc_v[...] = gv
            acc_k[...] = gk
        else:
            acc_v[...] += gv
            acc_k[...] += gk
        gq = dot(kt[...], g_high, NN) + dot(kt[...], g_low, NN)
        acc_q[b * HEAD : (b + 1) * HEAD, :] = gq[:HEAD] + gq[HEAD:]

    def packed(acc):
        x = acc[...]
        x = x + swap_halves(x)
        return jnp.where(low_half((half, LANES)), x[:half], x[half:]).reshape(n_seq, 8, LANES)

    ret[:, 16:24, :] = packed(acc_v)
    ret[:, 8:16, :] = packed(acc_k) * SCALE
    ret[:, 0:8, :] = (acc_q[...].T * SCALE).reshape(n_seq, 8, LANES)

    def raw_step(s, acc):
        g = [ret[s, 8 * m : 8 * m + 8, :] for m in range(3)]
        done = []
        for i in range(K):
            x = recv[s, 8 * i : 8 * i + 8, :]
            for m in range(3):
                done.append(acc[3 * i + m] + x * g[m])
        return tuple(done)

    zero = jnp.zeros((8, LANES), F32)
    acc = lax.fori_loop(0, n_seq, raw_step, (zero,) * (3 * K))
    for i in range(K):
        for m in range(3):
            r = K * m + i
            rows[r : r + 1, :] = jnp.sum(acc[3 * i + m], axis=0, keepdims=True)
    x = rows[...]
    x = x + swap_halves(x)
    low = low_half((8, LANES))
    dp_all[plane, 0:8] = jnp.where(low, x[0:8], x[8:16])
    dp_all[plane, 8:12] = jnp.where(low[:4], x[16:20], x[20:24])

    for k in range(1, n_dp):
        d = n_dp // 2 + (k // 2 if k % 2 else -(k // 2))
        other = lax.rem(plane + d, n_dp)
        pltpu.make_async_remote_copy(
            src_ref=dp_all.at[plane],
            dst_ref=dp_all.at[plane],
            send_sem=send_sem.at[2],
            recv_sem=recv_sem.at[2],
            device_id=(other, me),
            device_id_type=MESH,
        ).start()

    to_seq(lambda h: ret.at[h], back, 1, lambda k: recv_sem.at[1])
    pltpu.make_async_copy(ret.at[me], back.at[me], recv_sem.at[1]).start()

    others = dp_all.at[pl.ds(0, n_dp - 1)]
    pltpu.make_async_copy(others, others, recv_sem.at[2]).wait()
    total = jnp.sum(dp_all[...], axis=0)
    total_ref[...] = total
    squares_ref[me] = jnp.sum(total * total, axis=0, keepdims=True)
    to_seq(lambda h: squares_ref.at[me], squares_ref, 3, lambda k: recv_sem.at[3])

    arrived(back, recv_sem.at[1])

    def spread(t, _):
        lanes = pl.ds(pl.multiple_of(t * LANES, LANES), LANES)
        g = []
        for m in range(3):
            at = slice(8 * m, 8 * m + 8)
            g.append(jnp.concatenate(pair_up(back[2 * t, at], back[2 * t + 1, at]), axis=0))
        ws = [w[m, :, lanes] for m in range(3)]
        for j in range(GROUP):
            out_ref[0, 8 * j : 8 * j + 8, lanes] = (
                ws[0] * g[0][j : j + 1] + ws[1] * g[1][j : j + 1] + ws[2] * g[2][j : j + 1]
            )
        return 0

    lax.fori_loop(0, tiles, spread, 0)

    rest = squares_ref.at[pl.ds(0, n_seq - 1)]
    arrived(rest, recv_sem.at[3])
    for s, src in enumerate((send, ret, None, squares_ref)):
        src = others if src is None else src.at[pl.ds(0, n_seq - 1)]
        pltpu.make_async_copy(src, src, send_sem.at[s]).wait()


def main_call(tokens, cotangent, short_weights, n_seq, n_dp):
    tiles, sums = n_seq // 2, n_seq * GROUP
    vmem = pl.BlockSpec(memory_space=pltpu.VMEM)
    hbm = pl.BlockSpec(memory_space=pltpu.HBM)

    def v(*shape, dtype=F32):
        return pltpu.VMEM(shape, dtype)

    return pl.pallas_call(
        functools.partial(main_kernel, n_seq, n_dp),
        out_shape=(
            jax.ShapeDtypeStruct((1, GROUP * K, tiles * LANES), F32),
            jax.ShapeDtypeStruct((12, LANES), F32),
            jax.ShapeDtypeStruct((n_seq, 1, LANES), F32),
        ),
        in_specs=[hbm] * 3,
        out_specs=(vmem,) * 3,
        scratch_shapes=[
            v(tiles, GROUP * K, LANES), v(tiles, GROUP * K, LANES), v(3, K, tiles * LANES), v(3 * K, 8, LANES),
            v(n_seq, 8 * K + 8, LANES), v(n_seq, 8 * K + 8, LANES),
            v(sums, 256, dtype=BF16), v(sums, 256, dtype=BF16), v(sums, LANES, dtype=BF16),
            v(sums, 256, dtype=BF16), v(sums, 256, dtype=BF16), v(sums, LANES, dtype=BF16),
            v(sums, LANES), v(LANES, sums, dtype=BF16),
            v(sums, LANES), v(sums, LANES), v(LANES, sums // 2),
            v(n_seq, 24, LANES), v(n_seq, 24, LANES), v(3 * K, LANES), v(n_dp, 12, LANES),
            pltpu.SemaphoreType.DMA((2 * tiles + 1,)),
            pltpu.SemaphoreType.DMA((4,)),
            pltpu.SemaphoreType.DMA((tiles,)),
            pltpu.SemaphoreType.DMA((4,)),
        ],
        compiler_params=pltpu.CompilerParams(
            collective_id=0, has_side_effects=True, vmem_limit_bytes=40 * 2**20
        ),
        name="attend",
    )(tokens, cotangent, short_weights)


def last_kernel(entries, grads_ref, total_ref, squares_ref, out_ref, gw_ref, sem):
    pieces = sem.shape[0]
    rows = grads_ref.shape[1] // pieces
    copies = [
        pltpu.make_async_copy(
            grads_ref.at[0, pl.ds(r * rows, rows)], out_ref.at[0, pl.ds(r * rows, rows)], sem.at[r]
        )
        for r in range(pieces)
    ]
    for c in copies:
        c.start()
    mean_sq = jnp.full((8, LANES), jnp.sum(squares_ref[...]) / entries, F32)
    factor = jnp.minimum(1.0, 1.0 / jnp.sqrt(mean_sq + 1e-06))
    p = total_ref[0:8] * factor
    r = total_ref[8:12] * factor[:4]
    gw_ref[0] = p[:, :HEAD]
    gw_ref[1] = swap_halves(p)[:, :HEAD]
    gw_ref[2, 0:4] = r[:, :HEAD]
    gw_ref[2, 4:8] = swap_halves(r)[:, :HEAD]
    for c in copies:
        c.wait()


def last_call(grads, total, squares, entries):
    vmem = pl.BlockSpec(memory_space=pltpu.VMEM)
    return pl.pallas_call(
        functools.partial(last_kernel, entries),
        out_shape=(
            jax.ShapeDtypeStruct(grads.shape, F32),
            jax.ShapeDtypeStruct((3, K, HEAD), F32),
        ),
        in_specs=[vmem] * 3,
        out_specs=(pl.BlockSpec(memory_space=pltpu.HBM), vmem),
        scratch_shapes=[pltpu.SemaphoreType.DMA((8,))],
        compiler_params=pltpu.CompilerParams(vmem_limit_bytes=16 * 2**20),
        name="spread",
    )(grads, total, squares)


def solution(mesh):
    n_seq, n_dp = mesh.shape["seq"], mesh.shape["dp"]

    def per_device(tokens, cotangent, short_weights):
        grads, total, squares = main_call(tokens, cotangent, short_weights, n_seq, n_dp)
        return last_call(grads, total, squares, short_weights.size)

    return jax.shard_map(
        per_device,
        mesh=mesh,
        in_specs=(P("dp", "seq", None), P("dp", "seq", None), P()),
        out_specs=(P("dp", "seq", None), P(None, None, "seq")),
        check_vma=False,
    )
```

```python
import functools

import jax
import jax.numpy as jnp
from jax import lax
from jax.experimental import pallas as pl
from jax.experimental.pallas import tpu as pltpu
from jax.sharding import PartitionSpec as P

HEAD = 64
LANES = 128
K = 8
WIDE = 256
GROUP = 16
SCALE = HEAD ** (-0.5)
LOG2E = 1.4426950408889634
MESH = pl.DeviceIdType.MESH
STEPS = sorted(((a, b) for a in range(4) for b in range(4)), key=lambda t: min(t[0], 4 - t[0]) + min(t[1], 4 - t[1]))
FAR_FIRST = [(a, b, c) for a, b in STEPS[::-1] for c in range(2) if (a, b, c) != (0, 0, 0)]
NT = (((1,), (1,)), ((), ()))
NN = (((1,), (0,)), ((), ()))
F32, BF16 = jnp.float32, jnp.bfloat16


def low_half(shape):
    return lax.broadcasted_iota(jnp.int32, shape, len(shape) - 1) < HEAD


def swap_halves(x):
    return pltpu.roll(x, HEAD, len(x.shape) - 1)


def pair_up(x, y):
    low = low_half(x.shape)
    r = swap_halves(jnp.where(low, y, x))
    return jnp.where(low, x, r), jnp.where(low, r, y)


def both_halves(x):
    low = low_half(x.shape)
    r = swap_halves(x)
    return jnp.where(low, x, r), jnp.where(low, r, x)


def dot(a, b, dims):
    return lax.dot_general(a, b, dims, preferred_element_type=F32)


def two_parts(x):
    high = x.astype(BF16).astype(F32)
    return high, x - high


def main_kernel(
    n_seq, n_dp,
    tok_hbm, cot_hbm, w_hbm,
    out_ref, total_ref, squares_ref,
    tok, cot, w, wb,
    send, recv,
    qs, ks, qc, os, vs, oc, kc, kt,
    acc_k, acc_v, acc_q,
    ret, back, rows, dp_all,
    load_sem, send_sem, in_sem, recv_sem, relay,
):
    me = lax.axis_index("seq")
    plane = lax.axis_index("dp")
    tiles = n_seq // 2
    chip, core = me // 2, lax.rem(me, 2)
    cx, cy = chip // 4, lax.rem(chip, 4)
    sums = n_seq * GROUP
    half = sums // 2

    barrier = pltpu.get_barrier_semaphore()

    def hello_seq(d, _):
        other = lax.rem(me + d, n_seq)
        pl.semaphore_signal(barrier, inc=1, device_id=(plane, other), device_id_type=MESH)
        return 0

    def tell_planes(sem, d):
        for other in (lax.rem(plane + d, n_dp), lax.rem(plane + n_dp - d, n_dp)):
            pl.semaphore_signal(sem, inc=1, device_id=(other, me), device_id_type=MESH)

    lax.fori_loop(1, n_seq, hello_seq, 0)
    tell_planes(barrier, 1)

    def tile_loads(t):
        lanes = pl.ds(pl.multiple_of(t * LANES, LANES), LANES)
        return (
            pltpu.make_async_copy(tok_hbm.at[0, :, lanes], tok.at[t], load_sem.at[2 * t]),
            pltpu.make_async_copy(cot_hbm.at[0, :, lanes], cot.at[t], load_sem.at[2 * t + 1]),
        )

    def start_loads(t, _):
        for c in tile_loads(t):
            c.start()
        return 0

    lax.fori_loop(0, tiles, start_loads, 0)
    w_load = pltpu.make_async_copy(w_hbm, w, load_sem.at[2 * tiles])
    w_load.start()

    def pack(t, _):
        for c in tile_loads(t):
            c.wait()
        o = None
        for i in range(K):
            x = tok[t, pl.ds(i, GROUP, stride=K), :]
            c = cot[t, pl.ds(i, GROUP, stride=K), :]
            o = c if o is None else o + c
            even, odd = pair_up(x[:8], x[8:])
            send[2 * t, 8 * i : 8 * i + 8] = even
            send[2 * t + 1, 8 * i : 8 * i + 8] = odd
        even, odd = pair_up(o[:8], o[8:])
        send[2 * t, 8 * K : 8 * K + 8] = even
        send[2 * t + 1, 8 * K : 8 * K + 8] = odd
        return 0

    lax.fori_loop(0, tiles, pack, 0)

    w_load.wait()
    lanes = pl.ds(pl.multiple_of(chip * LANES, LANES), LANES)
    for m in range(3):
        first, second = both_halves(w[m, :, lanes])
        mine = jnp.where(core == 0, first, second)
        for i in range(K):
            wb[K * m + i] = jnp.broadcast_to(mine[i : i + 1], (8, LANES))

    pl.semaphore_wait(barrier, n_seq + 1)
    tell_planes(relay.at[0], 1)

    def to_seq(src_of, dst, s, sem_of):
        for a, b, c in FAR_FIRST:
            dx, dy = a + core * (b - a), b + core * (a - b)
            other = (((cx + dx) & 3) * 4 + ((cy + dy) & 3)) * 2 + (core ^ c)
            pltpu.make_async_remote_copy(
                src_ref=src_of(other),
                dst_ref=dst.at[me],
                send_sem=send_sem.at[s],
                recv_sem=sem_of(4 * dx + dy),
                device_id=(plane, other),
                device_id_type=MESH,
            ).start()

    def arrived(dst, sem):
        pltpu.make_async_copy(dst, dst, sem).wait()

    to_seq(lambda h: send.at[h], recv, 0, lambda k: in_sem.at[k])
    pltpu.make_async_copy(send.at[me], recv.at[me], in_sem.at[0]).start()
    pl.semaphore_wait(relay.at[0], 2)
    tell_planes(relay.at[1], 2)

    def query_role(x, side, cols, r0):
        for part, r in zip(both_halves(x), (r0, half + r0)):
            h, l = two_parts(part)
            at = pl.ds(pl.multiple_of(r, GROUP), GROUP)
            side[at, :LANES] = h.astype(BF16)
            side[at, LANES:] = l.astype(BF16)
            cols[at, :] = jnp.where(low_half(h.shape), h, l).astype(BF16)

    def key_role(x, side, r0, keep=None):
        for part, r in zip(both_halves(x), (r0, half + r0)):
            h, l = two_parts(part)
            at = pl.ds(pl.multiple_of(r, GROUP), GROUP)
            c = jnp.where(low_half(h.shape), h, l)
            side[at, :LANES] = c.astype(BF16)
            side[at, LANES:] = c.astype(BF16)
            if keep is not None:
                keep[at, :] = c

    def take(e, _):
        k = e ^ 10
        x, y = (cx - (k >> 2)) & 3, (cy - (k & 3)) & 3
        c = x * 4 + y
        block = recv.at[pl.ds(2 * c, 2)]
        arrived(block, in_sem.at[k])
        pooled = []
        for m in range(3):
            s = None
            for i in range(K):
                a = recv[pl.ds(2 * c, 2), 8 * i : 8 * i + 8, :] * wb[K * m + i]
                s = a if s is None else s + a
            pooled.append(s.reshape(GROUP, LANES))
        o = recv[pl.ds(2 * c, 2), 8 * K : 8 * K + 8, :].reshape(GROUP, LANES)
        r0 = c * GROUP
        query_role(pooled[0], qs, qc, r0)
        key_role(pooled[1], ks, r0, kc)
        key_role(pooled[2], vs, r0)
        query_role(o, os, oc, r0)
        return 0

    lax.fori_loop(0, tiles // 2, take, 0)
    pl.semaphore_wait(relay.at[1], 2)
    tell_planes(relay.at[2], 4)
    lax.fori_loop(tiles // 2, tiles, take, 0)

    kt[...] = kc[...].T.astype(BF16)
    for at in range(0, sums, WIDE):
        cols = slice(at, at + WIDE)
        s = dot(ks[...], qs[cols, :], NT)
        top = jnp.max(s, axis=0, keepdims=True)
        e = jnp.exp2((s - top) * (SCALE * LOG2E))
        p = e * (1.0 / jnp.sum(e, axis=0, keepdims=True))
        gp = dot(vs[...], os[cols, :], NT)
        delta = jnp.sum(p * gp, axis=0, keepdims=True)
        gs = p * (gp - delta)
        p_high, p_low = (x.astype(BF16) for x in two_parts(p))
        g_high, g_low = (x.astype(BF16) for x in two_parts(gs))
        gv = dot(p_high, oc[cols, :], NN) + dot(p_low, oc[cols, :], NN)
        gk = dot(g_high, qc[cols, :], NN) + dot(g_low, qc[cols, :], NN)
        if at == 0:
            acc_v[...] = gv
            acc_k[...] = gk
        else:
            acc_v[...] += gv
            acc_k[...] += gk
        gq = dot(kt[...], g_high, NN) + dot(kt[...], g_low, NN)
        first = HEAD * (at // half)
        acc_q[first : first + HEAD, at % half : at % half + WIDE] = gq[:HEAD] + gq[HEAD:]

    def packed(acc):
        x = acc[...]
        x = x + swap_halves(x)
        return jnp.where(low_half((half, LANES)), x[:half], x[half:]).reshape(n_seq, 8, LANES)

    ret[:, 16:24, :] = packed(acc_v)
    ret[:, 8:16, :] = packed(acc_k) * SCALE
    ret[:, 0:8, :] = (acc_q[...].T * SCALE).reshape(n_seq, 8, LANES)

    def raw_step(s, acc):
        g = [ret[s, 8 * m : 8 * m + 8, :] for m in range(3)]
        done = []
        for i in range(K):
            x = recv[s, 8 * i : 8 * i + 8, :]
            for m in range(3):
                done.append(acc[3 * i + m] + x * g[m])
        return tuple(done)

    zero = jnp.zeros((8, LANES), F32)
    acc = lax.fori_loop(0, n_seq, raw_step, (zero,) * (3 * K))
    for i in range(K):
        for m in range(3):
            r = K * m + i
            rows[r : r + 1, :] = jnp.sum(acc[3 * i + m], axis=0, keepdims=True)
    x = rows[...]
    x = x + swap_halves(x)
    low = low_half((8, LANES))
    dp_all[plane, 0:8] = jnp.where(low, x[0:8], x[8:16])
    dp_all[plane, 8:12] = jnp.where(low[:4], x[16:20], x[20:24])

    pl.semaphore_wait(relay.at[2], 2)
    for k in range(1, n_dp):
        d = n_dp // 2 + (k // 2 if k % 2 else -(k // 2))
        other = lax.rem(plane + d, n_dp)
        pltpu.make_async_remote_copy(
            src_ref=dp_all.at[plane],
            dst_ref=dp_all.at[plane],
            send_sem=send_sem.at[2],
            recv_sem=recv_sem.at[2],
            device_id=(other, me),
            device_id_type=MESH,
        ).start()

    to_seq(lambda h: ret.at[h], back, 1, lambda k: recv_sem.at[1])
    pltpu.make_async_copy(ret.at[me], back.at[me], recv_sem.at[1]).start()

    others = dp_all.at[pl.ds(0, n_dp - 1)]
    pltpu.make_async_copy(others, others, recv_sem.at[2]).wait()
    total = jnp.sum(dp_all[...], axis=0)
    total_ref[...] = total
    squares_ref[me] = jnp.sum(total * total, axis=0, keepdims=True)
    to_seq(lambda h: squares_ref.at[me], squares_ref, 3, lambda k: recv_sem.at[3])

    arrived(back, recv_sem.at[1])

    def spread(t, _):
        lanes = pl.ds(pl.multiple_of(t * LANES, LANES), LANES)
        g = []
        for m in range(3):
            at = slice(8 * m, 8 * m + 8)
            g.append(jnp.concatenate(pair_up(back[2 * t, at], back[2 * t + 1, at]), axis=0))
        ws = [w[m, :, lanes] for m in range(3)]
        for j in range(GROUP):
            out_ref[0, 8 * j : 8 * j + 8, lanes] = (
                ws[0] * g[0][j : j + 1] + ws[1] * g[1][j : j + 1] + ws[2] * g[2][j : j + 1]
            )
        return 0

    lax.fori_loop(0, tiles, spread, 0)

    rest = squares_ref.at[pl.ds(0, n_seq - 1)]
    arrived(rest, recv_sem.at[3])
    for s, src in enumerate((send, ret, None, squares_ref)):
        src = others if src is None else src.at[pl.ds(0, n_seq - 1)]
        pltpu.make_async_copy(src, src, send_sem.at[s]).wait()


def main_call(tokens, cotangent, short_weights, n_seq, n_dp):
    tiles, sums = n_seq // 2, n_seq * GROUP
    vmem = pl.BlockSpec(memory_space=pltpu.VMEM)
    hbm = pl.BlockSpec(memory_space=pltpu.HBM)

    def v(*shape, dtype=F32):
        return pltpu.VMEM(shape, dtype)

    return pl.pallas_call(
        functools.partial(main_kernel, n_seq, n_dp),
        out_shape=(
            jax.ShapeDtypeStruct((1, GROUP * K, tiles * LANES), F32),
            jax.ShapeDtypeStruct((12, LANES), F32),
            jax.ShapeDtypeStruct((n_seq, 1, LANES), F32),
        ),
        in_specs=[hbm] * 3,
        out_specs=(vmem,) * 3,
        scratch_shapes=[
            v(tiles, GROUP * K, LANES), v(tiles, GROUP * K, LANES), v(3, K, tiles * LANES), v(3 * K, 8, LANES),
            v(n_seq, 8 * K + 8, LANES), v(n_seq, 8 * K + 8, LANES),
            v(sums, 256, dtype=BF16), v(sums, 256, dtype=BF16), v(sums, LANES, dtype=BF16),
            v(sums, 256, dtype=BF16), v(sums, 256, dtype=BF16), v(sums, LANES, dtype=BF16),
            v(sums, LANES), v(LANES, sums, dtype=BF16),
            v(sums, LANES), v(sums, LANES), v(LANES, sums // 2),
            v(n_seq, 24, LANES), v(n_seq, 24, LANES), v(3 * K, LANES), v(n_dp, 12, LANES),
            pltpu.SemaphoreType.DMA((2 * tiles + 1,)),
            pltpu.SemaphoreType.DMA((4,)),
            pltpu.SemaphoreType.DMA((tiles,)),
            pltpu.SemaphoreType.DMA((4,)),
            pltpu.SemaphoreType.REGULAR((3,)),
        ],
        compiler_params=pltpu.CompilerParams(
            collective_id=0, has_side_effects=True, vmem_limit_bytes=40 * 2**20
        ),
        name="attend",
    )(*(pltpu.with_memory_space_constraint(x, pltpu.HBM) for x in (tokens, cotangent, short_weights)))


def last_kernel(entries, grads_ref, total_ref, squares_ref, out_ref, gw_ref, sem):
    pieces = sem.shape[0]
    rows = grads_ref.shape[1] // pieces
    copies = [
        pltpu.make_async_copy(
            grads_ref.at[0, pl.ds(r * rows, rows)], out_ref.at[0, pl.ds(r * rows, rows)], sem.at[r]
        )
        for r in range(pieces)
    ]
    for c in copies:
        c.start()
    mean_sq = jnp.full((8, LANES), jnp.sum(squares_ref[...]) / entries, F32)
    factor = jnp.minimum(1.0, 1.0 / jnp.sqrt(mean_sq + 1e-06))
    p = total_ref[0:8] * factor
    r = total_ref[8:12] * factor[:4]
    gw_ref[0] = p[:, :HEAD]
    gw_ref[1] = swap_halves(p)[:, :HEAD]
    gw_ref[2, 0:4] = r[:, :HEAD]
    gw_ref[2, 4:8] = swap_halves(r)[:, :HEAD]
    for c in copies:
        c.wait()


def last_call(grads, total, squares, entries):
    vmem = pl.BlockSpec(memory_space=pltpu.VMEM)
    return pl.pallas_call(
        functools.partial(last_kernel, entries),
        out_shape=(
            jax.ShapeDtypeStruct(grads.shape, F32),
            jax.ShapeDtypeStruct((3, K, HEAD), F32),
        ),
        in_specs=[vmem] * 3,
        out_specs=(pl.BlockSpec(memory_space=pltpu.HBM), vmem),
        scratch_shapes=[pltpu.SemaphoreType.DMA((8,))],
        compiler_params=pltpu.CompilerParams(vmem_limit_bytes=16 * 2**20),
        name="spread",
    )(grads, total, squares)


def solution(mesh):
    n_seq, n_dp = mesh.shape["seq"], mesh.shape["dp"]

    def per_device(tokens, cotangent, short_weights):
        grads, total, squares = main_call(tokens, cotangent, short_weights, n_seq, n_dp)
        return last_call(grads, total, squares, short_weights.size)

    return jax.shard_map(
        per_device,
        mesh=mesh,
        in_specs=(P("dp", "seq", None), P("dp", "seq", None), P()),
        out_specs=(P("dp", "seq", None), P(None, None, "seq")),
        check_vma=False,
    )
```

```python
import functools

import jax
import jax.numpy as jnp
from jax import lax
from jax.experimental import pallas as pl
from jax.experimental.pallas import tpu as pltpu
from jax.sharding import PartitionSpec as P

HEAD = 64
LANES = 128
K = 8
TOGETHER = 2
WIDE = 256
GROUP = 16
SCALE = HEAD ** (-0.5)
LOG2E = 1.4426950408889634
MESH = pl.DeviceIdType.MESH
STEPS = sorted(((a, b) for a in range(4) for b in range(4)), key=lambda t: min(t[0], 4 - t[0]) + min(t[1], 4 - t[1]))
FAR_FIRST = [(a, b, c) for a, b in STEPS[::-1] for c in range(2) if (a, b, c) != (0, 0, 0)]
NT = (((1,), (1,)), ((), ()))
NN = (((1,), (0,)), ((), ()))
F32, BF16 = jnp.float32, jnp.bfloat16


def low_half(shape):
    return lax.broadcasted_iota(jnp.int32, shape, len(shape) - 1) < HEAD


def swap_halves(x):
    return pltpu.roll(x, HEAD, len(x.shape) - 1)


def pair_up(x, y):
    low = low_half(x.shape)
    r = swap_halves(jnp.where(low, y, x))
    return jnp.where(low, x, r), jnp.where(low, r, y)


def both_halves(x):
    low = low_half(x.shape)
    r = swap_halves(x)
    return jnp.where(low, x, r), jnp.where(low, r, x)


def dot(a, b, dims):
    return lax.dot_general(a, b, dims, preferred_element_type=F32)


def two_parts(x):
    high = x.astype(BF16).astype(F32)
    return high, x - high


def main_kernel(
    n_seq, n_dp,
    tok_hbm, cot_hbm, w_hbm,
    out_ref, total_ref, squares_ref,
    tok, cot, w, wb,
    send, recv,
    qs, ks, qc, os, vs, oc, kc, kt,
    acc_k, acc_v, acc_q,
    ret, back, rows, dp_all,
    load_sem, send_sem, in_sem, recv_sem, relay,
):
    me = lax.axis_index("seq")
    plane = lax.axis_index("dp")
    tiles = n_seq // 2
    chip, core = me // 2, lax.rem(me, 2)
    cx, cy = chip // 4, lax.rem(chip, 4)
    sums = n_seq * GROUP
    half = sums // 2

    barrier = pltpu.get_barrier_semaphore()

    partners = []
    for a, b, c in FAR_FIRST:
        dx, dy = a + core * (b - a), b + core * (a - b)
        other = (((cx + dx) & 3) * 4 + ((cy + dy) & 3)) * 2 + (core ^ c)
        partners.append((4 * dx + dy, other))

    def tell_planes(sem, d):
        for other in (lax.rem(plane + d, n_dp), lax.rem(plane + n_dp - d, n_dp)):
            pl.semaphore_signal(sem, inc=1, device_id=(other, me), device_id_type=MESH)

    for _, other in partners:
        pl.semaphore_signal(barrier, inc=1, device_id=(plane, other), device_id_type=MESH)
    tell_planes(barrier, 1)

    def tile_loads(t):
        lanes = pl.ds(pl.multiple_of(t * LANES, LANES), LANES)
        return (
            pltpu.make_async_copy(tok_hbm.at[0, :, lanes], tok.at[t], load_sem.at[2 * t]),
            pltpu.make_async_copy(cot_hbm.at[0, :, lanes], cot.at[t], load_sem.at[2 * t + 1]),
        )

    def start_loads(t, _):
        for c in tile_loads(t):
            c.start()
        return 0

    lax.fori_loop(0, tiles, start_loads, 0)
    w_load = pltpu.make_async_copy(w_hbm, w, load_sem.at[2 * tiles])
    w_load.start()

    def pack(t, _):
        for c in tile_loads(t):
            c.wait()
        o = None
        for i in range(K):
            x = tok[t, pl.ds(i, GROUP, stride=K), :]
            c = cot[t, pl.ds(i, GROUP, stride=K), :]
            o = c if o is None else o + c
            even, odd = pair_up(x[:8], x[8:])
            send[2 * t, 8 * i : 8 * i + 8] = even
            send[2 * t + 1, 8 * i : 8 * i + 8] = odd
        even, odd = pair_up(o[:8], o[8:])
        send[2 * t, 8 * K : 8 * K + 8] = even
        send[2 * t + 1, 8 * K : 8 * K + 8] = odd
        return 0

    lax.fori_loop(0, tiles, pack, 0)

    w_load.wait()
    lanes = pl.ds(pl.multiple_of(chip * LANES, LANES), LANES)
    for m in range(3):
        first, second = both_halves(w[m, :, lanes])
        mine = jnp.where(core == 0, first, second)
        for i in range(K):
            wb[K * m + i] = jnp.broadcast_to(mine[i : i + 1], (8, LANES))

    pl.semaphore_wait(barrier, n_seq + 1)
    tell_planes(relay.at[0], 1)

    def to_seq(src_of, dst, s, sem_of):
        for k, other in partners:
            pltpu.make_async_remote_copy(
                src_ref=src_of(other),
                dst_ref=dst.at[me],
                send_sem=send_sem.at[s],
                recv_sem=sem_of(k),
                device_id=(plane, other),
                device_id_type=MESH,
            ).start()

    def arrived(dst, sem):
        pltpu.make_async_copy(dst, dst, sem).wait()

    to_seq(lambda h: send.at[h], recv, 0, lambda k: in_sem.at[k])
    pltpu.make_async_copy(send.at[me], recv.at[me], in_sem.at[0]).start()
    pl.semaphore_wait(relay.at[0], 2)
    tell_planes(relay.at[1], 2)
    pl.semaphore_wait(relay.at[1], 2)
    tell_planes(relay.at[2], 4)

    def query_role(x, side, cols, r0):
        for part, r in zip(both_halves(x), (r0, half + r0)):
            h, l = two_parts(part)
            at = pl.ds(pl.multiple_of(r, GROUP), GROUP)
            side[at, :LANES] = h.astype(BF16)
            side[at, LANES:] = l.astype(BF16)
            cols[at, :] = jnp.where(low_half(h.shape), h, l).astype(BF16)

    def key_role(x, side, r0, keep=None):
        for part, r in zip(both_halves(x), (r0, half + r0)):
            h, l = two_parts(part)
            at = pl.ds(pl.multiple_of(r, GROUP), GROUP)
            c = jnp.where(low_half(h.shape), h, l)
            side[at, :LANES] = c.astype(BF16)
            side[at, LANES:] = c.astype(BF16)
            if keep is not None:
                keep[at, :] = c

    def source(e):
        k = e ^ 10
        return k, ((cx - (k >> 2)) & 3) * 4 + ((cy - (k & 3)) & 3)

    def take(e, _):
        chips = []
        for k, c in (source(TOGETHER * e + n) for n in range(TOGETHER)):
            arrived(recv.at[pl.ds(2 * c, 2)], in_sem.at[k])
            chips.append(c)
        for c in chips:
            pooled = []
            for m in range(3):
                s = None
                for i in range(K):
                    a = recv[pl.ds(2 * c, 2), 8 * i : 8 * i + 8, :] * wb[K * m + i]
                    s = a if s is None else s + a
                pooled.append(s.reshape(GROUP, LANES))
            o = recv[pl.ds(2 * c, 2), 8 * K : 8 * K + 8, :].reshape(GROUP, LANES)
            r0 = c * GROUP
            query_role(pooled[0], qs, qc, r0)
            key_role(pooled[1], ks, r0, kc)
            key_role(pooled[2], vs, r0)
            query_role(o, os, oc, r0)
        return 0

    lax.fori_loop(0, tiles // TOGETHER, take, 0)

    kt[...] = kc[...].T.astype(BF16)
    for at in range(0, sums, WIDE):
        cols = slice(at, at + WIDE)
        s = dot(ks[...], qs[cols, :], NT)
        gp = dot(vs[...], os[cols, :], NT)
        top = jnp.max(s, axis=0, keepdims=True)
        e = jnp.exp2((s - top) * (SCALE * LOG2E))
        r = 1.0 / jnp.sum(e, axis=0, keepdims=True)
        delta = jnp.sum(e * gp, axis=0, keepdims=True) * r
        p = e * r
        gs = p * (gp - delta)
        p_high, p_low = (x.astype(BF16) for x in two_parts(p))
        g_high, g_low = (x.astype(BF16) for x in two_parts(gs))
        o, q, k = oc[cols, :], qc[cols, :], kt[...]
        gv = dot(jnp.concatenate([p_high, p_low], 1), jnp.concatenate([o, o], 0), NN)
        gk = dot(jnp.concatenate([g_high, g_low], 1), jnp.concatenate([q, q], 0), NN)
        if at == 0:
            acc_v[...] = gv
            acc_k[...] = gk
        else:
            acc_v[...] += gv
            acc_k[...] += gk
        gq = dot(jnp.concatenate([k, k], 1), jnp.concatenate([g_high, g_low], 0), NN)
        first = HEAD * (at // half)
        acc_q[first : first + HEAD, at % half : at % half + WIDE] = gq[:HEAD] + gq[HEAD:]

    def packed(acc):
        x = acc[...]
        x = x + swap_halves(x)
        return jnp.where(low_half((half, LANES)), x[:half], x[half:]).reshape(n_seq, 8, LANES)

    ret[:, 16:24, :] = packed(acc_v)
    ret[:, 8:16, :] = packed(acc_k) * SCALE
    ret[:, 0:8, :] = (acc_q[...].T * SCALE).reshape(n_seq, 8, LANES)

    def raw_step(s, acc):
        g = [ret[s, 8 * m : 8 * m + 8, :] for m in range(3)]
        done = []
        for i in range(K):
            x = recv[s, 8 * i : 8 * i + 8, :]
            for m in range(3):
                done.append(acc[3 * i + m] + x * g[m])
        return tuple(done)

    zero = jnp.zeros((8, LANES), F32)
    acc = lax.fori_loop(0, n_seq, raw_step, (zero,) * (3 * K), unroll=2)
    for i in range(K):
        for m in range(3):
            r = K * m + i
            rows[r : r + 1, :] = jnp.sum(acc[3 * i + m], axis=0, keepdims=True)
    x = rows[...]
    x = x + swap_halves(x)
    low = low_half((8, LANES))
    dp_all[plane, 0:8] = jnp.where(low, x[0:8], x[8:16])
    dp_all[plane, 8:12] = jnp.where(low[:4], x[16:20], x[20:24])

    pl.semaphore_wait(relay.at[2], 2)
    for k in range(n_dp - 1):
        other = k + (k >= plane).astype(jnp.int32)
        pltpu.make_async_remote_copy(
            src_ref=dp_all.at[plane],
            dst_ref=dp_all.at[plane],
            send_sem=send_sem.at[2],
            recv_sem=recv_sem.at[2],
            device_id=(other, me),
            device_id_type=MESH,
        ).start()

    to_seq(lambda h: ret.at[h], back, 1, lambda k: recv_sem.at[1])
    pltpu.make_async_copy(ret.at[me], back.at[me], recv_sem.at[1]).start()

    others = dp_all.at[pl.ds(0, n_dp - 1)]
    pltpu.make_async_copy(others, others, recv_sem.at[2]).wait()
    total = jnp.sum(dp_all[...], axis=0)
    total_ref[...] = total
    squares_ref[me] = jnp.sum(total * total, axis=0, keepdims=True)
    to_seq(lambda h: squares_ref.at[me], squares_ref, 3, lambda k: recv_sem.at[3])

    arrived(back, recv_sem.at[1])

    def spread(t, _):
        lanes = pl.ds(pl.multiple_of(t * LANES, LANES), LANES)
        g = []
        for m in range(3):
            at = slice(8 * m, 8 * m + 8)
            g.append(jnp.concatenate(pair_up(back[2 * t, at], back[2 * t + 1, at]), axis=0))
        ws = [w[m, :, lanes] for m in range(3)]
        for j in range(GROUP):
            out_ref[0, 8 * j : 8 * j + 8, lanes] = (
                ws[0] * g[0][j : j + 1] + ws[1] * g[1][j : j + 1] + ws[2] * g[2][j : j + 1]
            )
        return 0

    lax.fori_loop(0, tiles, spread, 0)

    rest = squares_ref.at[pl.ds(0, n_seq - 1)]
    arrived(rest, recv_sem.at[3])
    for s, src in enumerate((send, ret, None, squares_ref)):
        src = others if src is None else src.at[pl.ds(0, n_seq - 1)]
        pltpu.make_async_copy(src, src, send_sem.at[s]).wait()


def main_call(tokens, cotangent, short_weights, n_seq, n_dp):
    tiles, sums = n_seq // 2, n_seq * GROUP
    vmem = pl.BlockSpec(memory_space=pltpu.VMEM)
    hbm = pl.BlockSpec(memory_space=pltpu.HBM)

    def v(*shape, dtype=F32):
        return pltpu.VMEM(shape, dtype)

    return pl.pallas_call(
        functools.partial(main_kernel, n_seq, n_dp),
        out_shape=(
            jax.ShapeDtypeStruct((1, GROUP * K, tiles * LANES), F32),
            jax.ShapeDtypeStruct((12, LANES), F32),
            jax.ShapeDtypeStruct((n_seq, 1, LANES), F32),
        ),
        in_specs=[hbm] * 3,
        out_specs=(vmem,) * 3,
        scratch_shapes=[
            v(tiles, GROUP * K, LANES), v(tiles, GROUP * K, LANES), v(3, K, tiles * LANES), v(3 * K, 8, LANES),
            v(n_seq, 8 * K + 8, LANES), v(n_seq, 8 * K + 8, LANES),
            v(sums, 256, dtype=BF16), v(sums, 256, dtype=BF16), v(sums, LANES, dtype=BF16),
            v(sums, 256, dtype=BF16), v(sums, 256, dtype=BF16), v(sums, LANES, dtype=BF16),
            v(sums, LANES), v(LANES, sums, dtype=BF16),
            v(sums, LANES), v(sums, LANES), v(LANES, sums // 2),
            v(n_seq, 24, LANES), v(n_seq, 24, LANES), v(3 * K, LANES), v(n_dp, 12, LANES),
            pltpu.SemaphoreType.DMA((2 * tiles + 1,)),
            pltpu.SemaphoreType.DMA((4,)),
            pltpu.SemaphoreType.DMA((tiles,)),
            pltpu.SemaphoreType.DMA((4,)),
            pltpu.SemaphoreType.REGULAR((3,)),
        ],
        compiler_params=pltpu.CompilerParams(
            collective_id=0, has_side_effects=True, vmem_limit_bytes=40 * 2**20
        ),
        name="attend",
    )(*(pltpu.with_memory_space_constraint(x, pltpu.HBM) for x in (tokens, cotangent, short_weights)))


def last_kernel(entries, grads_ref, total_ref, squares_ref, out_ref, gw_ref, sem):
    pieces = sem.shape[0]
    rows = grads_ref.shape[1] // pieces
    copies = [
        pltpu.make_async_copy(
            grads_ref.at[0, pl.ds(r * rows, rows)], out_ref.at[0, pl.ds(r * rows, rows)], sem.at[r]
        )
        for r in range(pieces)
    ]
    for c in copies:
        c.start()
    mean_sq = jnp.full((8, LANES), jnp.sum(squares_ref[...]) / entries, F32)
    factor = jnp.minimum(1.0, 1.0 / jnp.sqrt(mean_sq + 1e-06))
    p = total_ref[0:8] * factor
    r = total_ref[8:12] * factor[:4]
    gw_ref[0] = p[:, :HEAD]
    gw_ref[1] = swap_halves(p)[:, :HEAD]
    gw_ref[2, 0:4] = r[:, :HEAD]
    gw_ref[2, 4:8] = swap_halves(r)[:, :HEAD]
    for c in copies:
        c.wait()


def last_call(grads, total, squares, entries):
    vmem = pl.BlockSpec(memory_space=pltpu.VMEM)
    return pl.pallas_call(
        functools.partial(last_kernel, entries),
        out_shape=(
            jax.ShapeDtypeStruct(grads.shape, F32),
            jax.ShapeDtypeStruct((3, K, HEAD), F32),
        ),
        in_specs=[vmem] * 3,
        out_specs=(pl.BlockSpec(memory_space=pltpu.HBM), vmem),
        scratch_shapes=[pltpu.SemaphoreType.DMA((8,))],
        compiler_params=pltpu.CompilerParams(vmem_limit_bytes=16 * 2**20),
        name="spread",
    )(grads, total, squares)


def solution(mesh):
    n_seq, n_dp = mesh.shape["seq"], mesh.shape["dp"]

    def per_device(tokens, cotangent, short_weights):
        grads, total, squares = main_call(tokens, cotangent, short_weights, n_seq, n_dp)
        return last_call(grads, total, squares, short_weights.size)

    return jax.shard_map(
        per_device,
        mesh=mesh,
        in_specs=(P("dp", "seq", None), P("dp", "seq", None), P()),
        out_specs=(P("dp", "seq", None), P(None, None, "seq")),
        check_vma=False,
    )
```

```python
import functools

import jax
import jax.numpy as jnp
from jax import lax
from jax.experimental import pallas as pl
from jax.experimental.pallas import tpu as pltpu
from jax.sharding import PartitionSpec as P

HEAD = 64
LANES = 128
K = 8
TOGETHER = 2
WIDE = 512
GROUP = 16
SCALE = HEAD ** (-0.5)
LOG2E = 1.4426950408889634
MESH = pl.DeviceIdType.MESH
STEPS = ((2, 2), (1, 2), (3, 2), (2, 1), (2, 3), (1, 1), (3, 3), (1, 3), (3, 1), (2, 0), (0, 2), (1, 0), (3, 0), (0, 1), (0, 3), (0, 0))
FAR_FIRST = [(a, b, c) for a, b in STEPS for c in range(2) if (a, b, c) != (0, 0, 0)]
NT = (((1,), (1,)), ((), ()))
NN = (((1,), (0,)), ((), ()))
F32, BF16 = jnp.float32, jnp.bfloat16


def low_half(shape):
    return lax.broadcasted_iota(jnp.int32, shape, len(shape) - 1) < HEAD


def swap_halves(x):
    return pltpu.roll(x, HEAD, len(x.shape) - 1)


def pair_up(x, y):
    low = low_half(x.shape)
    r = swap_halves(jnp.where(low, y, x))
    return jnp.where(low, x, r), jnp.where(low, r, y)


def both_halves(x):
    low = low_half(x.shape)
    r = swap_halves(x)
    return jnp.where(low, x, r), jnp.where(low, r, x)


def dot(a, b, dims):
    return lax.dot_general(a, b, dims, preferred_element_type=F32)


def two_parts(x):
    high = x.astype(BF16).astype(F32)
    return high, x - high


def main_kernel(
    n_seq, n_dp,
    tok_hbm, cot_hbm, w_hbm,
    out_ref, total_ref, squares_ref,
    tok, cot, w, wb,
    send, recv,
    qs, ks, qc, os, vs, oc, kc, kt,
    acc_k, acc_v, acc_q,
    ret, back, rows, dp_all,
    load_sem, send_sem, in_sem, recv_sem, relay,
):
    me = lax.axis_index("seq")
    plane = lax.axis_index("dp")
    tiles = n_seq // 2
    chip, core = me // 2, lax.rem(me, 2)
    cx, cy = chip // 4, lax.rem(chip, 4)
    sums = n_seq * GROUP
    half = sums // 2

    barrier = pltpu.get_barrier_semaphore()

    partners = []
    for a, b, c in FAR_FIRST:
        dx, dy = a + core * (b - a), b + core * (a - b)
        other = (((cx + dx) & 3) * 4 + ((cy + dy) & 3)) * 2 + (core ^ c)
        partners.append((4 * dx + dy, other))

    def tell_planes(sem, d):
        for other in (lax.rem(plane + d, n_dp), lax.rem(plane + n_dp - d, n_dp)):
            pl.semaphore_signal(sem, inc=1, device_id=(other, me), device_id_type=MESH)

    for _, other in partners:
        pl.semaphore_signal(barrier, inc=1, device_id=(plane, other), device_id_type=MESH)
    tell_planes(barrier, 1)

    def tile_loads(t):
        lanes = pl.ds(pl.multiple_of(t * LANES, LANES), LANES)
        return (
            pltpu.make_async_copy(tok_hbm.at[0, :, lanes], tok.at[t], load_sem.at[2 * t]),
            pltpu.make_async_copy(cot_hbm.at[0, :, lanes], cot.at[t], load_sem.at[2 * t + 1]),
        )

    def start_loads(t, _):
        for c in tile_loads(t):
            c.start()
        return 0

    lax.fori_loop(0, tiles, start_loads, 0)
    w_load = pltpu.make_async_copy(w_hbm, w, load_sem.at[2 * tiles])
    w_load.start()

    def pack(t, _):
        for c in tile_loads(t):
            c.wait()
        o = None
        for i in range(K):
            x = tok[t, pl.ds(i, GROUP, stride=K), :]
            c = cot[t, pl.ds(i, GROUP, stride=K), :]
            o = c if o is None else o + c
            even, odd = pair_up(x[:8], x[8:])
            send[2 * t, 8 * i : 8 * i + 8] = even
            send[2 * t + 1, 8 * i : 8 * i + 8] = odd
        even, odd = pair_up(o[:8], o[8:])
        send[2 * t, 8 * K : 8 * K + 8] = even
        send[2 * t + 1, 8 * K : 8 * K + 8] = odd
        return 0

    lax.fori_loop(0, tiles, pack, 0)

    w_load.wait()
    lanes = pl.ds(pl.multiple_of(chip * LANES, LANES), LANES)
    for m in range(3):
        first, second = both_halves(w[m, :, lanes])
        mine = jnp.where(core == 0, first, second)
        for i in range(K):
            wb[K * m + i] = jnp.broadcast_to(mine[i : i + 1], (8, LANES))

    pl.semaphore_wait(barrier, n_seq + 1)
    tell_planes(relay.at[0], 1)

    def to_seq(src_of, dst, s, sem_of):
        for k, other in partners:
            pltpu.make_async_remote_copy(
                src_ref=src_of(other),
                dst_ref=dst.at[me],
                send_sem=send_sem.at[s],
                recv_sem=sem_of(k),
                device_id=(plane, other),
                device_id_type=MESH,
            ).start()

    def arrived(dst, sem):
        pltpu.make_async_copy(dst, dst, sem).wait()

    to_seq(lambda h: send.at[h], recv, 0, lambda k: in_sem.at[k])
    pltpu.make_async_copy(send.at[me], recv.at[me], in_sem.at[0]).start()
    pl.semaphore_wait(relay.at[0], 2)
    tell_planes(relay.at[1], 2)
    pl.semaphore_wait(relay.at[1], 2)
    tell_planes(relay.at[2], 4)

    def query_role(x, side, cols, r0):
        for part, r in zip(both_halves(x), (r0, half + r0)):
            h, l = two_parts(part)
            at = pl.ds(pl.multiple_of(r, GROUP), GROUP)
            side[at, :LANES] = h.astype(BF16)
            side[at, LANES:] = l.astype(BF16)
            cols[at, :] = jnp.where(low_half(h.shape), h, l).astype(BF16)

    def key_role(x, side, r0, keep=None):
        for part, r in zip(both_halves(x), (r0, half + r0)):
            h, l = two_parts(part)
            at = pl.ds(pl.multiple_of(r, GROUP), GROUP)
            c = jnp.where(low_half(h.shape), h, l)
            side[at, :LANES] = c.astype(BF16)
            side[at, LANES:] = c.astype(BF16)
            if keep is not None:
                keep[at, :] = c

    def source(e):
        k = e ^ 10
        return k, ((cx - (k >> 2)) & 3) * 4 + ((cy - (k & 3)) & 3)

    def take(e, _):
        chips = []
        for k, c in (source(TOGETHER * e + n) for n in range(TOGETHER)):
            arrived(recv.at[pl.ds(2 * c, 2)], in_sem.at[k])
            chips.append(c)
        for c in chips:
            pooled = []
            for m in range(3):
                s = None
                for i in range(K):
                    a = recv[pl.ds(2 * c, 2), 8 * i : 8 * i + 8, :] * wb[K * m + i]
                    s = a if s is None else s + a
                pooled.append(s.reshape(GROUP, LANES))
            o = recv[pl.ds(2 * c, 2), 8 * K : 8 * K + 8, :].reshape(GROUP, LANES)
            r0 = c * GROUP
            query_role(pooled[0], qs, qc, r0)
            key_role(pooled[1], ks, r0, kc)
            key_role(pooled[2], vs, r0)
            query_role(o, os, oc, r0)
        return 0

    lax.fori_loop(0, tiles // TOGETHER, take, 0)

    kt[...] = kc[...].T.astype(BF16)
    for at in range(0, sums, WIDE):
        cols = slice(at, at + WIDE)
        s = dot(ks[...], qs[cols, :], NT)
        gp = dot(vs[...], os[cols, :], NT)
        top = jnp.max(s, axis=0, keepdims=True)
        e = jnp.exp2((s - top) * (SCALE * LOG2E))
        r = 1.0 / jnp.sum(e, axis=0, keepdims=True)
        delta = jnp.sum(e * gp, axis=0, keepdims=True) * r
        p = e * r
        gs = p * (gp - delta)
        p_high, p_low = (x.astype(BF16) for x in two_parts(p))
        g_high, g_low = (x.astype(BF16) for x in two_parts(gs))
        o, q, k = oc[cols, :], qc[cols, :], kt[...]
        gv = dot(jnp.concatenate([p_high, p_low], 1), jnp.concatenate([o, o], 0), NN)
        gk = dot(jnp.concatenate([g_high, g_low], 1), jnp.concatenate([q, q], 0), NN)
        if at == 0:
            acc_v[...] = gv
            acc_k[...] = gk
        else:
            acc_v[...] += gv
            acc_k[...] += gk
        gq = dot(jnp.concatenate([k, k], 1), jnp.concatenate([g_high, g_low], 0), NN)
        gq = gq[:HEAD] + gq[HEAD:]
        acc_q[:HEAD] = gq[:, :half]
        acc_q[HEAD:] = gq[:, half:]

    def packed(acc):
        x = acc[...]
        x = x + swap_halves(x)
        return jnp.where(low_half((half, LANES)), x[:half], x[half:]).reshape(n_seq, 8, LANES)

    ret[:, 16:24, :] = packed(acc_v)
    ret[:, 8:16, :] = packed(acc_k) * SCALE
    ret[:, 0:8, :] = (acc_q[...].T * SCALE).reshape(n_seq, 8, LANES)

    def raw_step(s, acc):
        g = [ret[s, 8 * m : 8 * m + 8, :] for m in range(3)]
        done = []
        for i in range(K):
            x = recv[s, 8 * i : 8 * i + 8, :]
            for m in range(3):
                done.append(acc[3 * i + m] + x * g[m])
        return tuple(done)

    zero = jnp.zeros((8, LANES), F32)
    acc = lax.fori_loop(0, n_seq, raw_step, (zero,) * (3 * K), unroll=4)
    for i in range(K):
        for m in range(3):
            r = K * m + i
            rows[r : r + 1, :] = jnp.sum(acc[3 * i + m], axis=0, keepdims=True)
    x = rows[...]
    x = x + swap_halves(x)
    low = low_half((8, LANES))
    dp_all[plane, 0:8] = jnp.where(low, x[0:8], x[8:16])
    dp_all[plane, 8:12] = jnp.where(low[:4], x[16:20], x[20:24])

    pl.semaphore_wait(relay.at[2], 2)
    for k in range(n_dp - 1):
        other = k + (k >= plane).astype(jnp.int32)
        pltpu.make_async_remote_copy(
            src_ref=dp_all.at[plane],
            dst_ref=dp_all.at[plane],
            send_sem=send_sem.at[2],
            recv_sem=recv_sem.at[2],
            device_id=(other, me),
            device_id_type=MESH,
        ).start()

    to_seq(lambda h: ret.at[h], back, 1, lambda k: recv_sem.at[1])
    pltpu.make_async_copy(ret.at[me], back.at[me], recv_sem.at[1]).start()

    others = dp_all.at[pl.ds(0, n_dp - 1)]
    pltpu.make_async_copy(others, others, recv_sem.at[2]).wait()
    total = jnp.sum(dp_all[...], axis=0)
    total_ref[...] = total
    squares_ref[me] = jnp.sum(total * total, axis=0, keepdims=True)
    to_seq(lambda h: squares_ref.at[me], squares_ref, 3, lambda k: recv_sem.at[3])

    arrived(back, recv_sem.at[1])

    def spread(t, _):
        lanes = pl.ds(pl.multiple_of(t * LANES, LANES), LANES)
        g = []
        for m in range(3):
            at = slice(8 * m, 8 * m + 8)
            g.append(jnp.concatenate(pair_up(back[2 * t, at], back[2 * t + 1, at]), axis=0))
        ws = [w[m, :, lanes] for m in range(3)]
        for j in range(GROUP):
            out_ref[0, 8 * j : 8 * j + 8, lanes] = (
                ws[0] * g[0][j : j + 1] + ws[1] * g[1][j : j + 1] + ws[2] * g[2][j : j + 1]
            )
        return 0

    lax.fori_loop(0, tiles, spread, 0)

    rest = squares_ref.at[pl.ds(0, n_seq - 1)]
    arrived(rest, recv_sem.at[3])
    for s, src in enumerate((send, ret, None, squares_ref)):
        src = others if src is None else src.at[pl.ds(0, n_seq - 1)]
        pltpu.make_async_copy(src, src, send_sem.at[s]).wait()


def main_call(tokens, cotangent, short_weights, n_seq, n_dp):
    tiles, sums = n_seq // 2, n_seq * GROUP
    vmem = pl.BlockSpec(memory_space=pltpu.VMEM)
    hbm = pl.BlockSpec(memory_space=pltpu.HBM)

    def v(*shape, dtype=F32):
        return pltpu.VMEM(shape, dtype)

    return pl.pallas_call(
        functools.partial(main_kernel, n_seq, n_dp),
        out_shape=(
            jax.ShapeDtypeStruct((1, GROUP * K, tiles * LANES), F32),
            jax.ShapeDtypeStruct((12, LANES), F32),
            jax.ShapeDtypeStruct((n_seq, 1, LANES), F32),
        ),
        in_specs=[hbm] * 3,
        out_specs=(vmem,) * 3,
        scratch_shapes=[
            v(tiles, GROUP * K, LANES), v(tiles, GROUP * K, LANES), v(3, K, tiles * LANES), v(3 * K, 8, LANES),
            v(n_seq, 8 * K + 8, LANES), v(n_seq, 8 * K + 8, LANES),
            v(sums, 256, dtype=BF16), v(sums, 256, dtype=BF16), v(sums, LANES, dtype=BF16),
            v(sums, 256, dtype=BF16), v(sums, 256, dtype=BF16), v(sums, LANES, dtype=BF16),
            v(sums, LANES), v(LANES, sums, dtype=BF16),
            v(sums, LANES), v(sums, LANES), v(LANES, sums // 2),
            v(n_seq, 24, LANES), v(n_seq, 24, LANES), v(3 * K, LANES), v(n_dp, 12, LANES),
            pltpu.SemaphoreType.DMA((2 * tiles + 1,)),
            pltpu.SemaphoreType.DMA((4,)),
            pltpu.SemaphoreType.DMA((tiles,)),
            pltpu.SemaphoreType.DMA((4,)),
            pltpu.SemaphoreType.REGULAR((3,)),
        ],
        compiler_params=pltpu.CompilerParams(
            collective_id=0, has_side_effects=True, vmem_limit_bytes=40 * 2**20
        ),
        name="attend",
    )(*(pltpu.with_memory_space_constraint(x, pltpu.HBM) for x in (tokens, cotangent, short_weights)))


def last_kernel(entries, grads_ref, total_ref, squares_ref, out_ref, gw_ref, sem):
    pieces = sem.shape[0]
    rows = grads_ref.shape[1] // pieces
    copies = [
        pltpu.make_async_copy(
            grads_ref.at[0, pl.ds(r * rows, rows)], out_ref.at[0, pl.ds(r * rows, rows)], sem.at[r]
        )
        for r in range(pieces)
    ]
    for c in copies:
        c.start()
    mean_sq = jnp.full((8, LANES), jnp.sum(squares_ref[...]) / entries, F32)
    factor = jnp.minimum(1.0, 1.0 / jnp.sqrt(mean_sq + 1e-06))
    p = total_ref[0:8] * factor
    r = total_ref[8:12] * factor[:4]
    gw_ref[0] = p[:, :HEAD]
    gw_ref[1] = swap_halves(p)[:, :HEAD]
    gw_ref[2, 0:4] = r[:, :HEAD]
    gw_ref[2, 4:8] = swap_halves(r)[:, :HEAD]
    for c in copies:
        c.wait()


def last_call(grads, total, squares, entries):
    vmem = pl.BlockSpec(memory_space=pltpu.VMEM)
    return pl.pallas_call(
        functools.partial(last_kernel, entries),
        out_shape=(
            jax.ShapeDtypeStruct(grads.shape, F32),
            jax.ShapeDtypeStruct((3, K, HEAD), F32),
        ),
        in_specs=[vmem] * 3,
        out_specs=(pl.BlockSpec(memory_space=pltpu.HBM), vmem),
        scratch_shapes=[pltpu.SemaphoreType.DMA((8,))],
        compiler_params=pltpu.CompilerParams(vmem_limit_bytes=16 * 2**20),
        name="spread",
    )(grads, total, squares)


def solution(mesh):
    n_seq, n_dp = mesh.shape["seq"], mesh.shape["dp"]

    def per_device(tokens, cotangent, short_weights):
        grads, total, squares = main_call(tokens, cotangent, short_weights, n_seq, n_dp)
        return last_call(grads, total, squares, short_weights.size)

    return jax.shard_map(
        per_device,
        mesh=mesh,
        in_specs=(P("dp", "seq", None), P("dp", "seq", None), P()),
        out_specs=(P("dp", "seq", None), P(None, None, "seq")),
        check_vma=False,
    )
```
